32 devices in a mesh: groups: 2 (over y), batch: 4 (over z), weight: 4 (over x, core).
Axes of the slice: x: 2, y: 2, z: 4, core: 2. Of those that a mesh axis runs over, the one named last changes fastest.
Arguments:
- tokens: bfloat16 [4096, 2048], P(('groups', 'batch'), 'weight'), parts along dimension 0, may hold values from -6 to 6
- gate_weight: bfloat16 [2048, 3072], P('batch', 'weight'), may hold values from -0.125 to 0.125
- up_weight: bfloat16 [2048, 3072], P('batch', 'weight'), may hold values from -0.125 to 0.125
- down_weight: bfloat16 [3072, 2048], P(None, ('weight', 'batch')), may hold values from -0.109375 to 0.109375
Outputs:
- layer_out: bfloat16 [4096, 2048], P(('groups', 'batch'), 'weight'), parts along dimension 0
The draws below stay inside these ranges and needn't reach their ends.
There are 2 independent parts, one for each index of `groups`. The reference program is written for one: setup_inputs(seed, part) draws one part's arguments, and reference() takes and returns one part's arrays. A program takes and returns all parts, laid end to end along the dimension named above; an argument that names none is the same for every part. Nothing has to cross between parts.
All inputs are finite; a program needn't handle non-finite values.
Results may differ from the reference program's by a relative error of at most 0.0051.
Values may be sent and summed in bfloat16 or wider, within the bound.
No kernel may reach another device: no remote copies, remote signals or barrier semaphores. Data moves between devices by JAX's collectives and lax.ppermute only.
A program may use at most 64 MiB of HBM per device.

```python
import jax
import jax.numpy as jnp

D = 2048
FF = 3072
TOKENS = 2048


def shard_levels(rng, shape, pieces, least, top_value):
    level, own = 1.0, jax.random.fold_in(rng, 6)
    for position, blocks in pieces:
        heights = jnp.exp(jax.random.uniform(jax.random.fold_in(own, position), (blocks,), jnp.float32, least / len(pieces), top_value / len(pieces)))
        level = level * jnp.repeat(heights, shape[position] // blocks).reshape([-1 if axis == position else 1 for axis in range(len(shape))])
    return level


def gaussian(key, extent, width, bound, split=(), kind=jnp.bfloat16):
    loudness = shard_levels(key, extent, split, -0.22, 0.18) if split else 1.0
    result = jax.random.normal(key, extent, jnp.float32) * width * loudness
    return jnp.minimum(jnp.maximum(result, -bound), bound).astype(kind)


def setup_inputs(seed: int = 0, part: int = 0) -> dict:
    streams_of = jax.random.split(jax.random.key(seed), 5)
    part_keys = jax.random.split(jax.random.fold_in(streams_of[4], part), 5)
    tokens = gaussian(part_keys[0], (TOKENS, D), 1.0, 6.0, ((0, 4), (1, 4)))
    gate_weight = gaussian(streams_of[1], (D, FF), D ** -0.5, 0.125, ((0, 4), (1, 4)))
    up_weight = gaussian(streams_of[2], (D, FF), D ** -0.5, 0.125, ((0, 4), (1, 4)))
    down_weight = gaussian(streams_of[3], (FF, D), FF ** -0.5, 0.109375, ((1, 16),))
    return dict(tokens=tokens, gate_weight=gate_weight, up_weight=up_weight, down_weight=down_weight)


def reference(tokens, gate_weight, up_weight, down_weight):
    gate_sum = jnp.dot(tokens, gate_weight, preferred_element_type=jnp.float32)
    up_sum = jnp.dot(tokens, up_weight, preferred_element_type=jnp.float32)
    hidden = (jax.nn.silu(gate_sum) * up_sum).astype(jnp.bfloat16)
    return jnp.dot(hidden, down_weight, preferred_element_type=jnp.float32).astype(jnp.bfloat16)
```

```python
import jax
import jax.numpy as jnp
from jax import lax
from jax.sharding import PartitionSpec as P

F32 = jnp.float32
BF16 = jnp.bfloat16


def dot(a, b):
    return jnp.dot(a, b, preferred_element_type=F32)


def after(value, *earlier):
    return lax.optimization_barrier((value, *earlier))[0]


def shards(sizes, tokens, gate_weight, up_weight, down_weight):
    n_batch, n_weight = sizes["batch"], sizes["weight"]
    plane = lax.axis_index("batch")
    place = lax.axis_index("weight")
    first = lax.axis_index("groups") == 0
    even = plane % 2 == 0
    rows, features = tokens.shape
    depth, units = gate_weight.shape
    half = units // 2
    columns = down_weight.shape[1]
    few = n_batch == n_weight == 4

    def flip(x, axis, bits):
        return lax.ppermute(x, axis, [(i, i ^ bits) for i in range(sizes[axis])])

    def own_half(weight):
        return jnp.where(even, weight[:, :half], weight[:, half:])

    def other_half(weight):
        return jnp.where(even, weight[:, half:], weight[:, :half])

    def sorted_pair(mine, theirs):
        return jnp.where(first, mine, theirs), jnp.where(first, theirs, mine)

    down_blocks = down_weight.reshape(n_weight, 2, half, columns)
    down_own = jnp.where(even, down_blocks[:, 0], down_blocks[:, 1])
    down_other = jnp.where(even, down_blocks[:, 1], down_blocks[:, 0])

    pair_rows = flip(tokens, "batch", 1)
    if few:
        tokens_x = flip(tokens, "weight", 2)

        send_own = jnp.where(first, own_half(gate_weight), own_half(up_weight))
        send_other = jnp.where(first, other_half(gate_weight), other_half(up_weight))
        keep_own = jnp.where(first, own_half(up_weight), own_half(gate_weight))
        direct = {0: send_own, 2: flip(send_own, "batch", 2), 1: flip(send_other, "batch", 1)}
        pair_x = flip(pair_rows, "weight", 2)
        direct[3] = flip(after(send_other, tokens_x), "batch", 3)
        swapped = {0: keep_own}
        for j in (1, 2, 3):
            swapped[j] = flip(direct[j], "groups", 1)

        near = jnp.concatenate([pair_rows, tokens], axis=0)
        far = jnp.concatenate([pair_x, tokens_x], axis=0)
        token_blocks = jnp.stack([near, flip(near, "weight", 1), far, flip(far, "weight", 1)])

        sums = [0.0, 0.0]
        for j in (0, 1, 2, 3):
            t = lax.dynamic_index_in_dim(token_blocks, place ^ plane ^ j, 0, keepdims=False)
            sums[0] += dot(t, direct[j])
            sums[1] += dot(t, swapped[j])

        low, high = slice(0, n_weight // 2), slice(n_weight // 2, n_weight)
        down_all = jnp.zeros((n_weight, half, n_batch * columns), BF16)
        down_all = lax.dynamic_update_slice(down_all, down_own, (0, 0, plane * columns))
        for j in (2, 3, 1):
            source = down_own if j == 2 else down_other
            part = jnp.where(first, source[low], source[high])
            mine = flip(after(part, swapped[1]), "batch", j)
            block = jnp.concatenate(sorted_pair(mine, flip(mine, "groups", 1)), axis=0)
            down_all = lax.dynamic_update_slice(down_all, block, (0, 0, (plane ^ j) * columns))
    else:
        both = lax.all_gather(jnp.concatenate([pair_rows, tokens], axis=0), "weight", axis=1, tiled=True)
        mine = lax.all_gather(jnp.where(first, gate_weight, up_weight), "batch", axis=0, tiled=True)
        mine = own_half(mine)
        sums = [dot(both, mine), dot(both, flip(mine, "groups", 1))]
        down_all = lax.all_gather(down_weight, "batch", axis=1, tiled=True)
        down_all = down_all.reshape(n_weight, 2, half, n_batch * columns)
        down_all = jnp.where(even, down_all[:, 0], down_all[:, 1])
    down_all = jnp.concatenate(
        [lax.dynamic_index_in_dim(down_all, place ^ i, 0, keepdims=False) for i in range(n_weight)], axis=0
    )

    def part_of_output(part):
        mine, theirs = (lax.slice_in_dim(s, part * rows, (part + 1) * rows) for s in sums)
        gate_sum, up_sum = sorted_pair(mine, theirs)
        hidden = (jax.nn.silu(gate_sum) * up_sum).astype(BF16)
        far = flip(hidden, "weight", 2)
        hidden = jnp.concatenate([hidden, flip(hidden, "weight", 1), far, flip(far, "weight", 1)], axis=1)
        return dot(hidden, down_all)

    theirs = flip(part_of_output(0).astype(BF16), "batch", 1)
    return (part_of_output(1) + theirs).astype(BF16)


def solution(mesh):
    in_specs = (
        P(("groups", "batch"), "weight"),
        P("batch", "weight"),
        P("batch", "weight"),
        P(None, ("weight", "batch")),
    )
    out_specs = P(("groups", "batch"), "weight")
    sizes = dict(mesh.shape)

    def body(*args):
        return shards(sizes, *args)

    return jax.shard_map(body, mesh=mesh, in_specs=in_specs, out_specs=out_specs, check_vma=False)
```

```python
import functools

import jax
import jax.numpy as jnp
from jax import lax
from jax.experimental import pallas as pl
from jax.experimental.pallas import tpu as pltpu
from jax.sharding import PartitionSpec as P

F32 = jnp.float32
BF16 = jnp.bfloat16
VMEM = pl.BlockSpec(memory_space=pltpu.VMEM)
SMEM = pl.BlockSpec(memory_space=pltpu.SMEM)


def dot(a, b):
    return jnp.dot(a, b, preferred_element_type=F32)


def nothing(token_ref, out_ref):
    del token_ref, out_ref


def span(token, cost):
    return pl.pallas_call(
        nothing,
        out_shape=jax.ShapeDtypeStruct((8, 128), F32),
        in_specs=[pl.BlockSpec(memory_space=pl.ANY)],
        out_specs=pl.BlockSpec(memory_space=pl.ANY),
        input_output_aliases={0: 0},
        cost_estimate=pl.CostEstimate(flops=cost, bytes_accessed=8192, transcendentals=0),
        compiler_params=pltpu.CompilerParams(has_side_effects=True),
    )(token)


def stage(token, *values, cost=5 * 10**8):
    token, *values = lax.optimization_barrier((token, *values))
    return span(token, cost), *values


def hidden_kernel(tile, at_ref, *refs):
    *refs, out_ref = refs
    n = len(refs) // 3
    blocks, direct, swapped = refs[:n], refs[n : 2 * n], refs[2 * n :]
    rows, units = out_ref.shape
    gate_first = at_ref[1] == 1
    for shift in range(n):

        @pl.when(at_ref[0] == shift)
        def _(shift=shift):
            parts = [jnp.concatenate([direct[j][...], swapped[j][...]], axis=1) for j in range(n)]
            weights = jnp.concatenate(parts, axis=0)
            for r in range(0, rows, tile):
                cut = pl.ds(r, tile)
                sums = dot(jnp.concatenate([blocks[shift ^ j][cut, :] for j in range(n)], axis=1), weights)
                a, b = sums[:, :units], sums[:, units:]
                gate, up = jnp.where(gate_first, a, b), jnp.where(gate_first, b, a)
                out_ref[cut, :] = (gate / (1.0 + jnp.exp(-gate)) * up).astype(BF16)


def hidden_of(at, blocks, direct, swapped):
    rows, units = blocks[0].shape[0], direct[0].shape[1]
    return pl.pallas_call(
        functools.partial(hidden_kernel, rows // 2),
        out_shape=jax.ShapeDtypeStruct((rows, units), BF16),
        in_specs=[SMEM] + [VMEM] * (len(blocks) + len(direct) + len(swapped)),
        out_specs=VMEM,
        cost_estimate=pl.CostEstimate(flops=10**6, bytes_accessed=10**4, transcendentals=0),
        compiler_params=pltpu.CompilerParams(vmem_limit_bytes=16 * 2**20),
    )(at, *blocks, *direct, *swapped)


def down_kernel(at_ref, own_ref, *refs):
    *parts, out_ref = refs
    n = len(parts) // 2
    columns = own_ref.shape[2]
    for b in range(own_ref.shape[0]):
        cut = pl.ds(pl.multiple_of(at_ref[1] * columns, columns), columns)
        out_ref[at_ref[0] ^ b, :, cut] = own_ref[b]
        for j in range(1, n + 1):
            cut = pl.ds(pl.multiple_of((at_ref[1] ^ j) * columns, columns), columns)
            value = parts[j - 1][b] if b < 2 else parts[n + j - 1][b - 2]
            out_ref[at_ref[0] ^ at_ref[2] ^ b, :, cut] = value


def gather_down(at, own, direct, swapped):
    blocks, half, columns = own.shape
    return pl.pallas_call(
        down_kernel,
        out_shape=jax.ShapeDtypeStruct((blocks, half, (len(direct) + 1) * columns), BF16),
        in_specs=[SMEM] + [VMEM] * (1 + len(direct) + len(swapped)),
        out_specs=VMEM,
        compiler_params=pltpu.CompilerParams(vmem_limit_bytes=16 * 2**20),
    )(at, own, *direct, *swapped)


def shards(sizes, tokens, gate_weight, up_weight, down_weight):
    n_batch, n_weight = sizes["batch"], sizes["weight"]
    plane = lax.axis_index("batch")
    place = lax.axis_index("weight")
    group = lax.axis_index("groups")
    first = group == 0
    parity = plane % 2
    even = parity == 0
    rows, features = tokens.shape
    depth, units = gate_weight.shape
    half = units // 2
    columns = down_weight.shape[1]

    def flip(x, axis, bits):
        return lax.ppermute(x, axis, [(i, i ^ bits) for i in range(sizes[axis])])

    def half_of(weight, parity):
        return lax.dynamic_slice_in_dim(weight, parity * half, half, axis=1)

    down_blocks = down_weight.reshape(n_weight, 2, half, columns)

    if n_batch == n_weight == 4:
        mine = jnp.where(first, gate_weight, up_weight)
        send_own, send_other = half_of(mine, parity), half_of(mine, 1 - parity)
        keep_own = half_of(jnp.where(first, up_weight, gate_weight), parity)
        low, high = slice(0, n_weight // 2), slice(n_weight // 2, n_weight)
        down_own = jnp.where(even, down_blocks[:, 0], down_blocks[:, 1])
        down_other = jnp.where(even, down_blocks[:, 1], down_blocks[:, 0])
        down_send = {
            j: jnp.where(first, source[low], source[high])
            for j, source in ((1, down_other), (2, down_own), (3, down_other))
        }

        token = jnp.zeros((8, 128), F32)
        tokens_x = flip(tokens, "weight", 2)
        tokens_pair = flip(tokens, "batch", 1)
        direct_2 = flip(send_own, "batch", 2)
        token, tokens_x, send_other = stage(token, tokens_x, send_other)
        direct_1 = flip(send_other, "batch", 1)
        token, tokens_pair, direct_2, send_other = stage(token, tokens_pair, direct_2, send_other)
        direct_3 = flip(send_other, "batch", 3)
        swapped_2 = flip(direct_2, "groups", 1)
        tokens_pair_x = flip(tokens_pair, "weight", 2)
        token, direct_1 = stage(token, direct_1, cost=2 * 10**9)
        swapped_1 = flip(direct_1, "groups", 1)
        token, tokens_pair_x, swapped_2, *own = stage(token, tokens_pair_x, swapped_2, tokens, tokens_x)
        own_core = [flip(x, "weight", 1) for x in own]
        pair_core = [flip(x, "weight", 1) for x in (tokens_pair, tokens_pair_x)]
        token, direct_3, *parts = stage(token, direct_3, down_send[1], down_send[2])
        swapped_3 = flip(direct_3, "groups", 1)
        down_direct = [flip(part, "batch", j) for j, part in zip((1, 2), parts)]
        token, swapped_1, part = stage(token, swapped_1, down_send[3], cost=2 * 10**9)
        down_direct.append(flip(part, "batch", 3))
        token, swapped_3, *cores = stage(token, swapped_3, *own_core, *pair_core)
        own_core, pair_core = cores[:2], cores[2:]
        at = jnp.stack([place ^ plane, jnp.where(first, 1, 0)]).astype(jnp.int32)
        direct = [send_own, direct_1, direct_2, direct_3]
        swapped = [keep_own, swapped_1, swapped_2, swapped_3]
        hidden_pair = hidden_of(at, [tokens_pair, pair_core[0], tokens_pair_x, pair_core[1]], direct, swapped)
        far_pair = flip(hidden_pair, "weight", 2)
        hidden_own = hidden_of(at, [tokens, own_core[0], tokens_x, own_core[1]], direct, swapped)
        token, hidden_own, down_direct[0], down_direct[1] = stage(
            token, hidden_own, down_direct[0], down_direct[1], cost=4 * 10**9
        )
        down_swapped = [flip(x, "groups", 1) for x in down_direct[:2]]
        token, down_direct[2] = stage(token, down_direct[2], cost=4 * 10**9)
        down_swapped.append(flip(down_direct[2], "groups", 1))
        token, far_pair, hidden_pair, hidden_own = stage(token, far_pair, hidden_pair, hidden_own)
        far_own = flip(hidden_own, "weight", 2)
        core_pair = [flip(x, "weight", 1) for x in (hidden_pair, far_pair)]
        token, down_swapped[0], down_swapped[1] = stage(token, down_swapped[0], down_swapped[1], cost=2 * 10**9)
        token, down_swapped[2] = stage(token, down_swapped[2], cost=3 * 10**9)
        at = jnp.stack([place, plane, jnp.where(first, 0, 2)]).astype(jnp.int32)
        down_all = gather_down(at, down_own, down_direct, down_swapped)
        token, *core_pair = stage(token, *core_pair)
    else:
        tokens_pair = flip(tokens, "batch", 1)
        both = lax.all_gather(jnp.concatenate([tokens_pair, tokens], axis=0), "weight", axis=1, tiled=True)
        mine = lax.all_gather(jnp.where(first, gate_weight, up_weight), "batch", axis=0, tiled=True)
        mine = half_of(mine, parity)
        mine, theirs = dot(both, mine), dot(both, flip(mine, "groups", 1))
        gate_sum, up_sum = jnp.where(first, mine, theirs), jnp.where(first, theirs, mine)
        hidden = (jax.nn.silu(gate_sum) * up_sum).astype(BF16)
        hidden_pair, hidden_own = hidden[:rows], hidden[rows:]
        far_pair, far_own = flip(hidden_pair, "weight", 2), flip(hidden_own, "weight", 2)
        core_pair = [flip(x, "weight", 1) for x in (hidden_pair, far_pair)]
        down_all = lax.all_gather(down_weight, "batch", axis=1, tiled=True)
        down_all = down_all.reshape(n_weight, 2, half, n_batch * columns)
        down_all = jnp.where(even, down_all[:, 0], down_all[:, 1])
        down_all = jnp.stack(
            [lax.dynamic_index_in_dim(down_all, place ^ i, 0, keepdims=False) for i in range(n_weight)]
        )

    down_all = down_all.reshape(n_weight * half, n_batch * columns)

    def output_of(hidden, far, core):
        return dot(jnp.concatenate([hidden, core[0], far, core[1]], axis=1), down_all)

    theirs = flip(output_of(hidden_pair, far_pair, core_pair).astype(BF16), "batch", 1)
    core_own = [flip(x, "weight", 1) for x in (hidden_own, far_own)]
    mine, theirs = lax.optimization_barrier((output_of(hidden_own, far_own, core_own), theirs))
    return (mine + theirs).astype(BF16)


def solution(mesh):
    in_specs = (
        P(("groups", "batch"), "weight"),
        P("batch", "weight"),
        P("batch", "weight"),
        P(None, ("weight", "batch")),
    )
    out_specs = P(("groups", "batch"), "weight")
    sizes = dict(mesh.shape)

    def body(*args):
        return shards(sizes, *args)

    return jax.shard_map(body, mesh=mesh, in_specs=in_specs, out_specs=out_specs, check_vma=False)
```

```python
import functools

import jax
import jax.numpy as jnp
from jax import lax
from jax.experimental import pallas as pl
from jax.experimental.pallas import tpu as pltpu
from jax.sharding import PartitionSpec as P

F32 = jnp.float32
BF16 = jnp.bfloat16
VMEM = pl.BlockSpec(memory_space=pltpu.VMEM)
SMEM = pl.BlockSpec(memory_space=pltpu.SMEM)


def dot(a, b):
    return jnp.dot(a, b, preferred_element_type=F32)


def nothing(token_ref, out_ref):
    del token_ref, out_ref


def span(token, cost):
    return pl.pallas_call(
        nothing,
        out_shape=jax.ShapeDtypeStruct((8, 128), F32),
        in_specs=[pl.BlockSpec(memory_space=pl.ANY)],
        out_specs=pl.BlockSpec(memory_space=pl.ANY),
        input_output_aliases={0: 0},
        cost_estimate=pl.CostEstimate(flops=cost, bytes_accessed=8192, transcendentals=0),
        compiler_params=pltpu.CompilerParams(has_side_effects=True),
    )(token)


def stage(token, *values, cost=5 * 10**8):
    token, *values = lax.optimization_barrier((token, *values))
    return span(token, cost), *values


def hidden_kernel(tile, at_ref, *refs):
    *refs, out_ref = refs
    n = len(refs) // 3
    blocks, direct, swapped = refs[:n], refs[n : 2 * n], refs[2 * n :]
    rows, units = out_ref.shape
    gate_first = at_ref[1] == 1
    for shift in range(n):

        @pl.when(at_ref[0] == shift)
        def _(shift=shift):
            parts = [jnp.concatenate([direct[j][...], swapped[j][...]], axis=1) for j in range(n)]
            weights = jnp.concatenate(parts, axis=0)
            for r in range(0, rows, tile):
                cut = pl.ds(r, tile)
                sums = dot(jnp.concatenate([blocks[shift ^ j][cut, :] for j in range(n)], axis=1), weights)
                a, b = sums[:, :units], sums[:, units:]
                gate, up = jnp.where(gate_first, a, b), jnp.where(gate_first, b, a)
                out_ref[cut, :] = (gate / (1.0 + jnp.exp(-gate)) * up).astype(BF16)


def hidden_of(at, blocks, direct, swapped):
    rows, units = blocks[0].shape[0], direct[0].shape[1]
    size = sum(x.size for x in (*blocks, *direct, *swapped)) * 2
    return pl.pallas_call(
        functools.partial(hidden_kernel, rows // 2),
        out_shape=jax.ShapeDtypeStruct((rows, units), BF16),
        in_specs=[SMEM] + [VMEM] * (len(blocks) + len(direct) + len(swapped)),
        out_specs=VMEM,
        cost_estimate=pl.CostEstimate(flops=0, bytes_accessed=size, transcendentals=0),
        compiler_params=pltpu.CompilerParams(vmem_limit_bytes=16 * 2**20),
    )(at, *blocks, *direct, *swapped)


def output_kernel(at_ref, *refs):
    n = 4
    hidden, refs, out_ref = refs[:n], refs[n:-1], refs[-1]
    whole = [ref for ref in refs if ref.shape[0] == n]
    split = [ref for ref in refs if ref.shape[0] != n]
    split = list(zip(split[::2], split[1::2]))
    for shift in range(n):

        @pl.when(at_ref[1] == shift)
        def _(shift=shift):
            parts = []
            for i in range(n):
                part = [ref[at_ref[0] ^ i] for ref in whole]
                b = shift ^ i
                part += [pair[b // (n // 2)][b % (n // 2)] for pair in split]
                parts.append(jnp.concatenate(part, axis=1) if len(part) > 1 else part[0])
            rows = jnp.concatenate([ref[...] for ref in hidden], axis=1)
            out_ref[...] = dot(rows, jnp.concatenate(parts, axis=0)).astype(out_ref.dtype)


def output_of(at, hidden, down, kind):
    columns = sum(part.shape[2] * part.shape[0] for part in down) // len(hidden)
    size = sum(x.size for x in (*hidden, *down)) * 2
    return pl.pallas_call(
        output_kernel,
        out_shape=jax.ShapeDtypeStruct((hidden[0].shape[0], columns), kind),
        in_specs=[SMEM] + [VMEM] * (len(hidden) + len(down)),
        out_specs=VMEM,
        cost_estimate=pl.CostEstimate(flops=0, bytes_accessed=size, transcendentals=0),
        compiler_params=pltpu.CompilerParams(vmem_limit_bytes=16 * 2**20),
    )(at, *hidden, *down)


def add_kernel(columns, at_ref, mine_ref, theirs_ref, out_ref):
    for j in range(out_ref.shape[1] // columns):
        mine, theirs = (pl.ds(i * columns, columns) for i in (j, j ^ 1))
        cut = pl.ds(pl.multiple_of((at_ref[0] ^ j) * columns, columns), columns)
        out_ref[:, cut] = (mine_ref[:, mine] + theirs_ref[:, theirs]).astype(BF16)


def add(at, columns, mine, theirs):
    return pl.pallas_call(
        functools.partial(add_kernel, columns),
        out_shape=jax.ShapeDtypeStruct(mine.shape, BF16),
        in_specs=[SMEM] + [VMEM] * 2,
        out_specs=VMEM,
        compiler_params=pltpu.CompilerParams(vmem_limit_bytes=16 * 2**20),
    )(at, mine, theirs)


def shards(sizes, tokens, gate_weight, up_weight, down_weight):
    n_batch, n_weight = sizes["batch"], sizes["weight"]
    plane = lax.axis_index("batch")
    place = lax.axis_index("weight")
    group = lax.axis_index("groups")
    first = group == 0
    parity = plane % 2
    even = parity == 0
    rows, features = tokens.shape
    depth, units = gate_weight.shape
    half = units // 2
    columns = down_weight.shape[1]

    def flip(x, axis, bits):
        return lax.ppermute(x, axis, [(i, i ^ bits) for i in range(sizes[axis])])

    def half_of(weight, parity):
        return lax.dynamic_slice_in_dim(weight, parity * half, half, axis=1)

    down_blocks = down_weight.reshape(n_weight, 2, half, columns)

    if n_batch == n_weight == 4:
        send_own = jnp.where(first, half_of(gate_weight, parity), half_of(up_weight, parity))
        token = jnp.zeros((8, 128), F32)
        tokens_x = flip(tokens, "weight", 2)
        tokens_pair = flip(tokens, "batch", 1)
        tokens_core = flip(tokens, "weight", 1)
        token, gate_weight, up_weight, send_own = stage(token, gate_weight, up_weight, send_own, cost=0)
        direct_2 = flip(send_own, "batch", 2)
        send_other = jnp.where(first, half_of(gate_weight, 1 - parity), half_of(up_weight, 1 - parity))
        keep_own = jnp.where(first, half_of(up_weight, parity), half_of(gate_weight, parity))
        low, high = slice(0, n_weight // 2), slice(n_weight // 2, n_weight)
        down_own = jnp.where(even, down_blocks[:, 0], down_blocks[:, 1])
        down_other = jnp.where(even, down_blocks[:, 1], down_blocks[:, 0])
        down_send_2 = jnp.where(first, down_own[low], down_own[high])
        down_send_3 = jnp.where(first, down_other[low], down_other[high])
        token, tokens_x, tokens_core, send_other = stage(token, tokens_x, tokens_core, send_other)
        direct_1 = flip(send_other, "batch", 1)
        token, tokens_pair, direct_2, send_other, tokens_x = stage(token, tokens_pair, direct_2, send_other, tokens_x)
        direct_3 = flip(send_other, "batch", 3)
        swapped_2 = flip(direct_2, "groups", 1)
        tokens_pair_x = flip(tokens_pair, "weight", 2)
        tokens_x_core = flip(tokens_x, "weight", 1)
        token, direct_1, keep_own, down_own, down_other, down_send_2, down_send_3 = stage(
            token, direct_1, keep_own, down_own, down_other, down_send_2, down_send_3, cost=2 * 10**9
        )
        swapped_1 = flip(direct_1, "groups", 1)
        token, tokens_pair_x, swapped_2, tokens_x_core = stage(token, tokens_pair_x, swapped_2, tokens_x_core)
        token, direct_3, x, y = stage(token, direct_3, tokens_pair, tokens_pair_x)
        swapped_3 = flip(direct_3, "groups", 1)
        pair_core = [flip(x, "weight", 1), flip(y, "weight", 1)]
        token, swapped_1, x, y = stage(token, swapped_1, down_other, down_send_2, cost=2 * 10**9)
        down_1 = flip(x, "batch", 1)
        down_2 = flip(y, "batch", 2)
        token, x, *pair_core = stage(token, down_send_3, *pair_core)
        down_3 = flip(x, "batch", 3)
        token, swapped_3 = stage(token, swapped_3, cost=0)
        at = jnp.stack([place ^ plane, jnp.where(first, 1, 0)]).astype(jnp.int32)
        direct = [send_own, direct_1, direct_2, direct_3]
        swapped = [keep_own, swapped_1, swapped_2, swapped_3]
        hidden_pair = hidden_of(at, [tokens_pair, pair_core[0], tokens_pair_x, pair_core[1]], direct, swapped)
        far_pair = flip(hidden_pair, "weight", 2)
        token, hidden_pair = stage(token, hidden_pair, cost=0)
        token, down_2, x = stage(token, down_2, tokens)
        swapped_down_2 = flip(down_2, "groups", 1)
        hidden_own = hidden_of(at, [x, tokens_core, tokens_x, tokens_x_core], direct, swapped)
        token, down_1, down_3, hidden_own = stage(token, down_1, down_3, hidden_own, cost=45 * 10**8)
        swapped_down_3 = flip(down_3, "groups", 1)
        token, far_pair, hidden_pair = stage(token, far_pair, hidden_pair)
        core_pair = [flip(x, "weight", 1) for x in (hidden_pair, far_pair)]
        far_own = flip(hidden_own, "weight", 2)
        token, swapped_down_2 = stage(token, swapped_down_2)
        token, swapped_down_3 = stage(token, swapped_down_3, cost=3 * 10**9)
        token, *core_pair = stage(token, *core_pair)
        at = jnp.stack([place, place ^ jnp.where(first, 0, 2)]).astype(jnp.int32)
        down = [down_own, down_1, down_2, swapped_down_2, down_3, swapped_down_3]
        part = output_of(at, [hidden_pair, core_pair[0], far_pair, core_pair[1]], down, BF16)
        theirs = flip(part, "batch", 1)
        token, far_own, x = stage(token, far_own, hidden_own)
        core_own = [flip(x, "weight", 1) for x in (x, far_own)]
        token, *core_own = stage(token, *core_own)
        mine = output_of(at, [hidden_own, core_own[0], far_own, core_own[1]], down, F32)
        token, mine, theirs = stage(token, mine, theirs)
        return add(plane.astype(jnp.int32).reshape(1), columns, mine, theirs)

    tokens_pair = flip(tokens, "batch", 1)
    both = lax.all_gather(jnp.concatenate([tokens_pair, tokens], axis=0), "weight", axis=1, tiled=True)
    mine = lax.all_gather(jnp.where(first, gate_weight, up_weight), "batch", axis=0, tiled=True)
    mine = half_of(mine, parity)
    mine, theirs = dot(both, mine), dot(both, flip(mine, "groups", 1))
    gate_sum, up_sum = jnp.where(first, mine, theirs), jnp.where(first, theirs, mine)
    hidden = lax.all_gather((jax.nn.silu(gate_sum) * up_sum).astype(BF16), "weight", axis=1, tiled=True)
    down_all = lax.all_gather(down_weight, "batch", axis=1, tiled=True)
    down_all = down_all.reshape(n_weight, 2, half, n_batch * columns)
    down_all = jnp.where(even, down_all[:, 0], down_all[:, 1]).reshape(n_weight * half, n_batch * columns)
    theirs = flip(dot(hidden[:rows], down_all).astype(BF16), "batch", 1)
    return (dot(hidden[rows:], down_all) + theirs).astype(BF16)


def solution(mesh):
    in_specs = (
        P(("groups", "batch"), "weight"),
        P("batch", "weight"),
        P("batch", "weight"),
        P(None, ("weight", "batch")),
    )
    out_specs = P(("groups", "batch"), "weight")
    sizes = dict(mesh.shape)

    def body(*args):
        return shards(sizes, *args)

    return jax.shard_map(body, mesh=mesh, in_specs=in_specs, out_specs=out_specs, check_vma=False)
```

```python
import functools

import jax
import jax.numpy as jnp
from jax import lax
from jax.experimental import pallas as pl
from jax.experimental.pallas import tpu as pltpu
from jax.sharding import PartitionSpec as P

F32 = jnp.float32
BF16 = jnp.bfloat16
VMEM = pl.BlockSpec(memory_space=pltpu.VMEM)
SMEM = pl.BlockSpec(memory_space=pltpu.SMEM)


def dot(a, b):
    return jnp.dot(a, b, preferred_element_type=F32)


def nothing(token_ref, out_ref):
    del token_ref, out_ref


def span(token, cost):
    return pl.pallas_call(
        nothing,
        out_shape=jax.ShapeDtypeStruct((8, 128), F32),
        in_specs=[pl.BlockSpec(memory_space=pl.ANY)],
        out_specs=pl.BlockSpec(memory_space=pl.ANY),
        input_output_aliases={0: 0},
        cost_estimate=pl.CostEstimate(flops=cost, bytes_accessed=8192, transcendentals=0),
        compiler_params=pltpu.CompilerParams(has_side_effects=True, vmem_limit_bytes=2**16),
    )(token)


def stage(token, *values, cost=5 * 10**8):
    token, *values = lax.optimization_barrier((token, *values))
    return span(token, cost), *values


def hidden_kernel(tile, at_ref, *refs):
    *refs, out_ref = refs
    n = len(refs) // 3
    blocks, direct, swapped = refs[:n], refs[n : 2 * n], refs[2 * n :]
    rows, units = out_ref.shape
    gate_first = at_ref[1] == 1
    for shift in range(n):

        @pl.when(at_ref[0] == shift)
        def _(shift=shift):
            parts = [jnp.concatenate([direct[j][...], swapped[j][...]], axis=1) for j in range(n)]
            weights = jnp.concatenate(parts, axis=0)
            for r in range(0, rows, tile):
                cut = pl.ds(r, tile)
                sums = dot(jnp.concatenate([blocks[shift ^ j][cut, :] for j in range(n)], axis=1), weights)
                a, b = sums[:, :units], sums[:, units:]
                gate, up = jnp.where(gate_first, a, b), jnp.where(gate_first, b, a)
                out_ref[cut, :] = (gate / (1.0 + jnp.exp(-gate)) * up).astype(BF16)


def hidden_of(at, blocks, direct, swapped):
    rows, units = blocks[0].shape[0], direct[0].shape[1]
    size = sum(x.size for x in (*blocks, *direct, *swapped)) * 2
    return pl.pallas_call(
        functools.partial(hidden_kernel, rows // 2),
        out_shape=jax.ShapeDtypeStruct((rows, units), BF16),
        in_specs=[SMEM] + [VMEM] * (len(blocks) + len(direct) + len(swapped)),
        out_specs=VMEM,
        cost_estimate=pl.CostEstimate(flops=0, bytes_accessed=size, transcendentals=0),
        compiler_params=pltpu.CompilerParams(vmem_limit_bytes=16 * 2**20),
    )(at, *blocks, *direct, *swapped)


def output_kernel(at_ref, *refs):
    n = 4
    hidden, refs, out_ref = refs[:n], refs[n:-1], refs[-1]
    whole = [ref for ref in refs if ref.shape[0] == n]
    split = [ref for ref in refs if ref.shape[0] != n]
    split = list(zip(split[::2], split[1::2]))
    for shift in range(n):

        @pl.when(at_ref[1] == shift)
        def _(shift=shift):
            parts = []
            for i in range(n):
                part = [ref[at_ref[0] ^ i] for ref in whole]
                b = shift ^ i
                part += [pair[b // (n // 2)][b % (n // 2)] for pair in split]
                parts.append(jnp.concatenate(part, axis=1) if len(part) > 1 else part[0])
            rows = jnp.concatenate([ref[...] for ref in hidden], axis=1)
            out_ref[...] = dot(rows, jnp.concatenate(parts, axis=0)).astype(out_ref.dtype)


def output_of(at, hidden, down, kind):
    columns = sum(part.shape[2] * part.shape[0] for part in down) // len(hidden)
    size = sum(x.size for x in (*hidden, *down)) * 2
    return pl.pallas_call(
        output_kernel,
        out_shape=jax.ShapeDtypeStruct((hidden[0].shape[0], columns), kind),
        in_specs=[SMEM] + [VMEM] * (len(hidden) + len(down)),
        out_specs=VMEM,
        cost_estimate=pl.CostEstimate(flops=0, bytes_accessed=size, transcendentals=0),
        compiler_params=pltpu.CompilerParams(vmem_limit_bytes=16 * 2**20),
    )(at, *hidden, *down)


def add_kernel(columns, at_ref, mine_ref, theirs_ref, out_ref):
    for j in range(out_ref.shape[1] // columns):
        mine, theirs = (pl.ds(i * columns, columns) for i in (j, j ^ 1))
        cut = pl.ds(pl.multiple_of((at_ref[0] ^ j) * columns, columns), columns)
        out_ref[:, cut] = (mine_ref[:, mine] + theirs_ref[:, theirs]).astype(BF16)


def add(at, columns, mine, theirs):
    return pl.pallas_call(
        functools.partial(add_kernel, columns),
        out_shape=jax.ShapeDtypeStruct(mine.shape, BF16),
        in_specs=[SMEM] + [VMEM] * 2,
        out_specs=VMEM,
        compiler_params=pltpu.CompilerParams(vmem_limit_bytes=16 * 2**20),
    )(at, mine, theirs)


def shards(sizes, tokens, gate_weight, up_weight, down_weight):
    n_batch, n_weight = sizes["batch"], sizes["weight"]
    plane = lax.axis_index("batch")
    place = lax.axis_index("weight")
    group = lax.axis_index("groups")
    first = group == 0
    parity = plane % 2
    even = parity == 0
    rows, features = tokens.shape
    depth, units = gate_weight.shape
    half = units // 2
    columns = down_weight.shape[1]

    def flip(x, axis, bits):
        return lax.ppermute(x, axis, [(i, i ^ bits) for i in range(sizes[axis])])

    def half_of(weight, parity):
        return lax.dynamic_slice_in_dim(weight, parity * half, half, axis=1)

    down_blocks = down_weight.reshape(n_weight, 2, half, columns)

    if n_batch == n_weight == 4:
        send_own = jnp.where(first, half_of(gate_weight, parity), half_of(up_weight, parity))
        token = jnp.zeros((8, 128), F32)
        tokens_x = flip(tokens, "weight", 2)
        tokens_pair = flip(tokens, "batch", 1)
        tokens_core = flip(tokens, "weight", 1)
        token, gate_weight, up_weight, send_own = stage(token, gate_weight, up_weight, send_own, cost=0)
        direct_2 = flip(send_own, "batch", 2)
        send_other = jnp.where(first, half_of(gate_weight, 1 - parity), half_of(up_weight, 1 - parity))
        keep_own = jnp.where(first, half_of(up_weight, parity), half_of(gate_weight, parity))
        low, high = slice(0, n_weight // 2), slice(n_weight // 2, n_weight)
        down_own = jnp.where(even, down_blocks[:, 0], down_blocks[:, 1])
        down_other = jnp.where(even, down_blocks[:, 1], down_blocks[:, 0])
        down_send_2 = jnp.where(first, down_own[low], down_own[high])
        down_send_3 = jnp.where(first, down_other[low], down_other[high])
        token, tokens_x, tokens_core, send_other = stage(token, tokens_x, tokens_core, send_other)
        direct_1 = flip(send_other, "batch", 1)
        token, tokens_pair, direct_2, send_other, tokens_x = stage(token, tokens_pair, direct_2, send_other, tokens_x)
        direct_3 = flip(send_other, "batch", 3)
        swapped_2 = flip(direct_2, "groups", 1)
        tokens_pair_x = flip(tokens_pair, "weight", 2)
        tokens_x_core = flip(tokens_x, "weight", 1)
        token, direct_1, keep_own, down_own, down_other, down_send_2, down_send_3 = stage(
            token, direct_1, keep_own, down_own, down_other, down_send_2, down_send_3, cost=2 * 10**9
        )
        swapped_1 = flip(direct_1, "groups", 1)
        token, tokens_pair_x, swapped_2, tokens_x_core = stage(token, tokens_pair_x, swapped_2, tokens_x_core)
        token, direct_3, x, y = stage(token, direct_3, tokens_pair, tokens_pair_x)
        swapped_3 = flip(direct_3, "groups", 1)
        pair_core = [flip(x, "weight", 1), flip(y, "weight", 1)]
        token, swapped_1, x, y = stage(token, swapped_1, down_other, down_send_2, cost=2 * 10**9)
        down_1 = flip(x, "batch", 1)
        down_2 = flip(y, "batch", 2)
        token, x, *pair_core = stage(token, down_send_3, *pair_core)
        down_3 = flip(x, "batch", 3)
        token, swapped_3 = stage(token, swapped_3, cost=0)
        at = jnp.stack([place ^ plane, jnp.where(first, 1, 0)]).astype(jnp.int32)
        direct = [send_own, direct_1, direct_2, direct_3]
        swapped = [keep_own, swapped_1, swapped_2, swapped_3]
        hidden_pair = hidden_of(at, [tokens_pair, pair_core[0], tokens_pair_x, pair_core[1]], direct, swapped)
        far_pair = flip(hidden_pair, "weight", 2)
        token, hidden_pair = stage(token, hidden_pair, cost=0)
        token, down_2, x = stage(token, down_2, tokens)
        swapped_down_2 = flip(down_2, "groups", 1)
        hidden_own = hidden_of(at, [x, tokens_core, tokens_x, tokens_x_core], direct, swapped)
        token, down_1, down_3, hidden_own = stage(token, down_1, down_3, hidden_own, cost=45 * 10**8)
        swapped_down_3 = flip(down_3, "groups", 1)
        token, far_pair, hidden_pair = stage(token, far_pair, hidden_pair)
        core_pair = [flip(x, "weight", 1) for x in (hidden_pair, far_pair)]
        far_own = flip(hidden_own, "weight", 2)
        token, swapped_down_2 = stage(token, swapped_down_2)
        token, swapped_down_3 = stage(token, swapped_down_3, cost=3 * 10**9)
        token, *core_pair = stage(token, *core_pair)
        at = jnp.stack([place, place ^ jnp.where(first, 0, 2)]).astype(jnp.int32)
        down = [down_own, down_1, down_2, swapped_down_2, down_3, swapped_down_3]
        part = output_of(at, [hidden_pair, core_pair[0], far_pair, core_pair[1]], down, BF16)
        theirs = flip(part, "batch", 1)
        token, far_own, x = stage(token, far_own, hidden_own)
        core_own = [flip(x, "weight", 1) for x in (x, far_own)]
        token, *core_own = stage(token, *core_own)
        mine = output_of(at, [hidden_own, core_own[0], far_own, core_own[1]], down, F32)
        token, mine, theirs = stage(token, mine, theirs)
        return add(plane.astype(jnp.int32).reshape(1), columns, mine, theirs)

    tokens_pair = flip(tokens, "batch", 1)
    both = lax.all_gather(jnp.concatenate([tokens_pair, tokens], axis=0), "weight", axis=1, tiled=True)
    mine = lax.all_gather(jnp.where(first, gate_weight, up_weight), "batch", axis=0, tiled=True)
    mine = half_of(mine, parity)
    mine, theirs = dot(both, mine), dot(both, flip(mine, "groups", 1))
    gate_sum, up_sum = jnp.where(first, mine, theirs), jnp.where(first, theirs, mine)
    hidden = lax.all_gather((jax.nn.silu(gate_sum) * up_sum).astype(BF16), "weight", axis=1, tiled=True)
    down_all = lax.all_gather(down_weight, "batch", axis=1, tiled=True)
    down_all = down_all.reshape(n_weight, 2, half, n_batch * columns)
    down_all = jnp.where(even, down_all[:, 0], down_all[:, 1]).reshape(n_weight * half, n_batch * columns)
    theirs = flip(dot(hidden[:rows], down_all).astype(BF16), "batch", 1)
    return (dot(hidden[rows:], down_all) + theirs).astype(BF16)


def solution(mesh):
    in_specs = (
        P(("groups", "batch"), "weight"),
        P("batch", "weight"),
        P("batch", "weight"),
        P(None, ("weight", "batch")),
    )
    out_specs = P(("groups", "batch"), "weight")
    sizes = dict(mesh.shape)

    def body(*args):
        return shards(sizes, *args)

    return jax.shard_map(body, mesh=mesh, in_specs=in_specs, out_specs=out_specs, check_vma=False)
```

```python
import functools

import jax
import jax.numpy as jnp
from jax import lax
from jax.experimental import pallas as pl
from jax.experimental.pallas import tpu as pltpu
from jax.sharding import PartitionSpec as P

F32 = jnp.float32
BF16 = jnp.bfloat16
VMEM = pl.BlockSpec(memory_space=pltpu.VMEM)
SMEM = pl.BlockSpec(memory_space=pltpu.SMEM)
ANY = pl.BlockSpec(memory_space=pl.ANY)

TRANSFERS = dict(
    tokens_x=("tokens", "weight", 2),
    tokens_core=("tokens", "weight", 1),
    tokens_x_core=("tokens_x", "weight", 1),
    pair=("tokens", "batch", 1),
    pair_x=("pair", "weight", 2),
    pair_core=("pair", "weight", 1),
    pair_x_core=("pair_x", "weight", 1),
    direct_1=("send_other", "batch", 1),
    direct_2=("send_own", "batch", 2),
    direct_3=("send_other", "batch", 3),
    swapped_1=("direct_1", "groups", 1),
    swapped_2=("direct_2", "groups", 1),
    swapped_3=("direct_3", "groups", 1),
    down_1=("down_other", "batch", 1),
    down_2=("down_send_2", "batch", 2),
    down_3=("down_send_3", "batch", 3),
    down_swapped_2=("down_2", "groups", 1),
    down_swapped_3=("down_3", "groups", 1),
    hidden_pair_x=("hidden_pair", "weight", 2),
    hidden_pair_core=("hidden_pair", "weight", 1),
    hidden_pair_x_core=("hidden_pair_x", "weight", 1),
    hidden_own_x=("hidden_own", "weight", 2),
    hidden_own_core=("hidden_own", "weight", 1),
    hidden_own_x_core=("hidden_own_x", "weight", 1),
    theirs=("part", "batch", 1),
)
PARTS = ("keep_own", "down_own", "down_other", "down_send_2", "down_send_3")
LATE = ("hidden_pair", "hidden_own", "part")
STAGES = (
    ((), ("tokens_x", "pair", "tokens_core"), None),
    (("gate_weight", "up_weight"), ("direct_2",), 0),
    (("tokens_x", "tokens_core"), ("direct_1",), 500),
    (("pair", "direct_2"), ("direct_3", "swapped_2", "pair_x", "tokens_x_core"), 500),
    (("direct_1", *PARTS), ("swapped_1",), 2600),
    (("pair_x", "swapped_2", "tokens_x_core"), (), 500),
    (("direct_3",), ("swapped_3", "pair_core", "pair_x_core"), 500),
    (("swapped_1",), ("down_1", "down_2"), 2000),
    (("pair_core", "pair_x_core"), ("down_3",), 500),
    (("swapped_3",), ("hidden_pair_x",), 0),
    (("hidden_pair",), (), 0),
    (("down_2",), ("down_swapped_2",), 500),
    (("down_1", "down_3", "hidden_own"), ("down_swapped_3",), 4500),
    (("hidden_pair_x",), ("hidden_pair_core", "hidden_pair_x_core", "hidden_own_x"), 500),
    (("down_swapped_2",), (), 500),
    (("down_swapped_3",), (), 3000),
    (("hidden_pair_core", "hidden_pair_x_core"), ("theirs",), 500),
    (("hidden_own_x",), ("hidden_own_core", "hidden_own_x_core"), 500),
    (("hidden_own_core", "hidden_own_x_core"), (), 500),
    (("mine", "theirs"), (), 500),
)


def dot(a, b):
    return jnp.dot(a, b, preferred_element_type=F32)


def nothing(token_ref, out_ref):
    del token_ref, out_ref


def span(token, cost):
    return pl.pallas_call(
        nothing,
        out_shape=jax.ShapeDtypeStruct((8, 128), F32),
        in_specs=[ANY],
        out_specs=ANY,
        input_output_aliases={0: 0},
        cost_estimate=pl.CostEstimate(flops=cost, bytes_accessed=8192, transcendentals=0),
        compiler_params=pltpu.CompilerParams(has_side_effects=True, vmem_limit_bytes=2**16),
    )(token)


def hidden_kernel(tile, at_ref, *refs):
    *refs, out_ref = refs
    n = len(refs) // 3
    blocks, direct, swapped = refs[:n], refs[n : 2 * n], refs[2 * n :]
    rows, units = out_ref.shape
    gate_first = at_ref[1] == 1
    for shift in range(n):

        @pl.when(at_ref[0] == shift)
        def _(shift=shift):
            parts = [jnp.concatenate([direct[j][...], swapped[j][...]], axis=1) for j in range(n)]
            weights = jnp.concatenate(parts, axis=0)
            for r in range(0, rows, tile):
                cut = pl.ds(r, tile)
                sums = dot(jnp.concatenate([blocks[shift ^ j][cut, :] for j in range(n)], axis=1), weights)
                a, b = sums[:, :units], sums[:, units:]
                gate, up = jnp.where(gate_first, a, b), jnp.where(gate_first, b, a)
                out_ref[cut, :] = (gate / (1.0 + jnp.exp(-gate)) * up).astype(BF16)


def hidden_of(at, blocks, direct, swapped):
    rows, units = blocks[0].shape[0], direct[0].shape[1]
    size = sum(x.size for x in (*blocks, *direct, *swapped)) * 2
    return pl.pallas_call(
        functools.partial(hidden_kernel, rows // 2),
        out_shape=jax.ShapeDtypeStruct((rows, units), BF16),
        in_specs=[SMEM] + [VMEM] * (len(blocks) + len(direct) + len(swapped)),
        out_specs=VMEM,
        cost_estimate=pl.CostEstimate(flops=0, bytes_accessed=size, transcendentals=0),
        compiler_params=pltpu.CompilerParams(vmem_limit_bytes=16 * 2**20),
    )(at, *blocks, *direct, *swapped)


def output_kernel(at_ref, *refs):
    n = 4
    hidden, refs, out_ref = refs[:n], refs[n:-1], refs[-1]
    whole = [ref for ref in refs if ref.shape[0] == n]
    split = [ref for ref in refs if ref.shape[0] != n]
    split = list(zip(split[::2], split[1::2]))
    for shift in range(n):

        @pl.when(at_ref[1] == shift)
        def _(shift=shift):
            parts = []
            for i in range(n):
                part = [ref[at_ref[0] ^ i] for ref in whole]
                b = shift ^ i
                part += [pair[b // (n // 2)][b % (n // 2)] for pair in split]
                parts.append(jnp.concatenate(part, axis=1) if len(part) > 1 else part[0])
            rows = jnp.concatenate([ref[...] for ref in hidden], axis=1)
            out_ref[...] = dot(rows, jnp.concatenate(parts, axis=0)).astype(out_ref.dtype)


def output_of(at, hidden, down, kind):
    columns = sum(part.shape[2] * part.shape[0] for part in down) // len(hidden)
    size = sum(x.size for x in (*hidden, *down)) * 2
    return pl.pallas_call(
        output_kernel,
        out_shape=jax.ShapeDtypeStruct((hidden[0].shape[0], columns), kind),
        in_specs=[SMEM] + [VMEM] * (len(hidden) + len(down)),
        out_specs=VMEM,
        cost_estimate=pl.CostEstimate(flops=0, bytes_accessed=size, transcendentals=0),
        compiler_params=pltpu.CompilerParams(vmem_limit_bytes=16 * 2**20),
    )(at, *hidden, *down)


def add_kernel(columns, at_ref, mine_ref, theirs_ref, out_ref):
    for j in range(out_ref.shape[1] // columns):
        mine, theirs = (pl.ds(i * columns, columns) for i in (j, j ^ 1))
        cut = pl.ds(pl.multiple_of((at_ref[0] ^ j) * columns, columns), columns)
        out_ref[:, cut] = (mine_ref[:, mine] + theirs_ref[:, theirs]).astype(BF16)


def add(at, columns, mine, theirs):
    return pl.pallas_call(
        functools.partial(add_kernel, columns),
        out_shape=jax.ShapeDtypeStruct(mine.shape, BF16),
        in_specs=[SMEM] + [VMEM] * 2,
        out_specs=VMEM,
        compiler_params=pltpu.CompilerParams(vmem_limit_bytes=16 * 2**20),
    )(at, mine, theirs)


def shards(sizes, tokens, gate_weight, up_weight, down_weight):
    n_batch, n_weight = sizes["batch"], sizes["weight"]
    plane = lax.axis_index("batch")
    place = lax.axis_index("weight")
    first = lax.axis_index("groups") == 0
    parity = plane % 2
    even = parity == 0
    rows = tokens.shape[0]
    half = gate_weight.shape[1] // 2
    columns = down_weight.shape[1]

    def flip(x, axis, bits):
        return lax.ppermute(x, axis, [(i, i ^ bits) for i in range(sizes[axis])])

    def half_of(weight, parity):
        return lax.dynamic_slice_in_dim(weight, parity * half, half, axis=1)

    def one_of(mine, theirs, parity):
        return jnp.where(first, half_of(mine, parity), half_of(theirs, parity))

    if n_batch == n_weight == 4:
        have = dict(tokens=tokens, gate_weight=gate_weight, up_weight=up_weight)
        have["send_own"] = one_of(gate_weight, up_weight, parity)
        blocks = down_weight.reshape(n_weight, 2, half, columns)
        low, high = slice(0, n_weight // 2), slice(n_weight // 2, n_weight)

        def names(kind):
            return [have[f"{kind}_{j}"] for j in (1, 2, 3)]

        def hidden(kind):
            at = jnp.stack([place ^ plane, jnp.where(first, 1, 0)]).astype(jnp.int32)
            tokens = [have[kind], have[f"{kind}_core"], have[f"{kind}_x"], have[f"{kind}_x_core"]]
            direct = [have["send_own"], *names("direct")]
            return hidden_of(at, tokens, direct, [have["keep_own"], *names("swapped")])

        def output(kind, type):
            at = jnp.stack([place, place ^ jnp.where(first, 0, 2)]).astype(jnp.int32)
            kind = f"hidden_{kind}"
            hidden = [have[kind], have[f"{kind}_core"], have[f"{kind}_x"], have[f"{kind}_x_core"]]
            down = [have["down_own"], have["down_1"]]
            for j in (2, 3):
                down += [have[f"down_{j}"], have[f"down_swapped_{j}"]]
            return output_of(at, hidden, down, type)

        results = dict(
            send_other=lambda: one_of(have["gate_weight"], have["up_weight"], 1 - parity),
            keep_own=lambda: one_of(have["up_weight"], have["gate_weight"], parity),
            down_own=lambda: jnp.where(even, blocks[:, 0], blocks[:, 1]),
            down_other=lambda: jnp.where(even, blocks[:, 1], blocks[:, 0]),
            down_send_2=lambda: jnp.where(first, get("down_own")[low], get("down_own")[high]),
            down_send_3=lambda: jnp.where(first, get("down_other")[low], get("down_other")[high]),
            hidden_pair=lambda: hidden("pair"),
            hidden_own=lambda: hidden("tokens"),
            part=lambda: output("pair", BF16),
            mine=lambda: output("own", F32),
        )

        def get(name):
            if name not in have:
                have[name] = results[name]()
            return have[name]

        token = jnp.zeros((8, 128), F32)
        for arrived, leaving, cost in STAGES:
            sent = [TRANSFERS[name][0] for name in leaving]
            held = dict.fromkeys((*arrived, *sent))
            held = {name: get(name) for name in held if name in arrived or name not in LATE}
            if cost is not None:
                token, *values = lax.optimization_barrier((token, *held.values()))
                held = dict(zip(held, values))
                have.update((name, held[name]) for name in arrived)
                token = span(token, cost * 10**6)
            for name in leaving:
                source, *way = TRANSFERS[name]
                have[name] = flip(held[source] if source in held else get(source), *way)
        return add(plane.astype(jnp.int32).reshape(1), columns, have["mine"], have["theirs"])

    tokens_pair = flip(tokens, "batch", 1)
    both = lax.all_gather(jnp.concatenate([tokens_pair, tokens], axis=0), "weight", axis=1, tiled=True)
    mine = lax.all_gather(jnp.where(first, gate_weight, up_weight), "batch", axis=0, tiled=True)
    mine = half_of(mine, parity)
    mine, theirs = dot(both, mine), dot(both, flip(mine, "groups", 1))
    gate_sum, up_sum = jnp.where(first, mine, theirs), jnp.where(first, theirs, mine)
    hidden = lax.all_gather((jax.nn.silu(gate_sum) * up_sum).astype(BF16), "weight", axis=1, tiled=True)
    down_all = lax.all_gather(down_weight, "batch", axis=1, tiled=True)
    down_all = down_all.reshape(n_weight, 2, half, n_batch * columns)
    down_all = jnp.where(even, down_all[:, 0], down_all[:, 1]).reshape(n_weight * half, n_batch * columns)
    theirs = flip(dot(hidden[:rows], down_all).astype(BF16), "batch", 1)
    return (dot(hidden[rows:], down_all) + theirs).astype(BF16)


def solution(mesh):
    in_specs = (
        P(("groups", "batch"), "weight"),
        P("batch", "weight"),
        P("batch", "weight"),
        P(None, ("weight", "batch")),
    )
    out_specs = P(("groups", "batch"), "weight")
    sizes = dict(mesh.shape)

    def body(*args):
        return shards(sizes, *args)

    return jax.shard_map(body, mesh=mesh, in_specs=in_specs, out_specs=out_specs, check_vma=False)
```

```python
import enum
import functools

import jax
import jax.numpy as jnp
from jax import lax
from jax.experimental import pallas as pl
from jax.experimental.pallas import tpu as pltpu
from jax.sharding import PartitionSpec as P

F32 = jnp.float32
BF16 = jnp.bfloat16
VMEM = pl.BlockSpec(memory_space=pltpu.VMEM)
SMEM = pl.BlockSpec(memory_space=pltpu.SMEM)
ANY = pl.BlockSpec(memory_space=pl.ANY)

BATCH, GROUPS, WEIGHT = "batch", "groups", "weight"


class N(enum.Enum):
    tokens = enum.auto()
    gate_weight = enum.auto()
    up_weight = enum.auto()
    send_own = enum.auto()
    send_other = enum.auto()
    keep_own = enum.auto()
    down_own = enum.auto()
    down_other = enum.auto()
    down_send_2 = enum.auto()
    down_send_3 = enum.auto()
    tokens_x = enum.auto()
    tokens_core = enum.auto()
    tokens_x_core = enum.auto()
    pair = enum.auto()
    pair_x = enum.auto()
    pair_core = enum.auto()
    pair_x_core = enum.auto()
    direct_1 = enum.auto()
    direct_2 = enum.auto()
    direct_3 = enum.auto()
    swapped_1 = enum.auto()
    swapped_2 = enum.auto()
    swapped_3 = enum.auto()
    down_1 = enum.auto()
    down_2 = enum.auto()
    down_3 = enum.auto()
    down_swapped_2 = enum.auto()
    down_swapped_3 = enum.auto()
    hidden_pair = enum.auto()
    hidden_pair_x = enum.auto()
    hidden_pair_core = enum.auto()
    hidden_pair_x_core = enum.auto()
    hidden_own = enum.auto()
    hidden_own_x = enum.auto()
    hidden_own_core = enum.auto()
    hidden_own_x_core = enum.auto()
    part = enum.auto()
    mine = enum.auto()
    theirs = enum.auto()


TRANSFERS = {
    N.tokens_x: (N.tokens, WEIGHT, 2),
    N.tokens_core: (N.tokens, WEIGHT, 1),
    N.tokens_x_core: (N.tokens_x, WEIGHT, 1),
    N.pair: (N.tokens, BATCH, 1),
    N.pair_x: (N.pair, WEIGHT, 2),
    N.pair_core: (N.pair, WEIGHT, 1),
    N.pair_x_core: (N.pair_x, WEIGHT, 1),
    N.direct_1: (N.send_other, BATCH, 1),
    N.direct_2: (N.send_own, BATCH, 2),
    N.direct_3: (N.send_other, BATCH, 3),
    N.swapped_1: (N.direct_1, GROUPS, 1),
    N.swapped_2: (N.direct_2, GROUPS, 1),
    N.swapped_3: (N.direct_3, GROUPS, 1),
    N.down_1: (N.down_other, BATCH, 1),
    N.down_2: (N.down_send_2, BATCH, 2),
    N.down_3: (N.down_send_3, BATCH, 3),
    N.down_swapped_2: (N.down_2, GROUPS, 1),
    N.down_swapped_3: (N.down_3, GROUPS, 1),
    N.hidden_pair_x: (N.hidden_pair, WEIGHT, 2),
    N.hidden_pair_core: (N.hidden_pair, WEIGHT, 1),
    N.hidden_pair_x_core: (N.hidden_pair_x, WEIGHT, 1),
    N.hidden_own_x: (N.hidden_own, WEIGHT, 2),
    N.hidden_own_core: (N.hidden_own, WEIGHT, 1),
    N.hidden_own_x_core: (N.hidden_own_x, WEIGHT, 1),
    N.theirs: (N.part, BATCH, 1),
}
PARTS = (N.keep_own, N.down_own, N.down_other, N.down_send_2, N.down_send_3)
LATE = (N.hidden_pair, N.hidden_own, N.part)
OWN = (N.tokens, N.tokens_core, N.tokens_x, N.tokens_x_core)
PAIR = (N.pair, N.pair_core, N.pair_x, N.pair_x_core)
HIDDEN_OWN = (N.hidden_own, N.hidden_own_core, N.hidden_own_x, N.hidden_own_x_core)
HIDDEN_PAIR = (N.hidden_pair, N.hidden_pair_core, N.hidden_pair_x, N.hidden_pair_x_core)
DIRECT = (N.send_own, N.direct_1, N.direct_2, N.direct_3)
SWAPPED = (N.keep_own, N.swapped_1, N.swapped_2, N.swapped_3)
DOWN = (N.down_own, N.down_1, N.down_2, N.down_swapped_2, N.down_3, N.down_swapped_3)
STAGES = (
    ((), (N.tokens_x, N.pair, N.tokens_core), None),
    ((N.gate_weight, N.up_weight), (N.direct_2,), 0),
    ((N.tokens_x, N.tokens_core), (N.direct_1,), 500),
    ((N.pair, N.direct_2), (N.direct_3, N.swapped_2, N.pair_x, N.tokens_x_core), 500),
    ((N.direct_1, *PARTS), (N.swapped_1,), 2600),
    ((N.pair_x, N.swapped_2, N.tokens_x_core), (), 500),
    ((N.direct_3,), (N.swapped_3, N.pair_core, N.pair_x_core), 500),
    ((N.swapped_1,), (N.down_1, N.down_2), 2000),
    ((N.pair_core, N.pair_x_core), (N.down_3,), 500),
    ((N.swapped_3,), (N.hidden_pair_x,), 0),
    ((N.hidden_pair,), (), 0),
    ((N.down_2,), (N.down_swapped_2,), 500),
    ((N.down_1, N.down_3, N.hidden_own), (N.down_swapped_3,), 4500),
    ((N.hidden_pair_x,), (N.hidden_pair_core, N.hidden_pair_x_core, N.hidden_own_x), 500),
    ((N.down_swapped_2,), (), 500),
    ((N.down_swapped_3,), (), 3000),
    ((N.hidden_pair_core, N.hidden_pair_x_core), (N.theirs,), 500),
    ((N.hidden_own_x,), (N.hidden_own_core, N.hidden_own_x_core), 500),
    ((N.hidden_own_core, N.hidden_own_x_core), (), 500),
    ((N.mine, N.theirs), (), 500),
)


def dot(a, b):
    return jnp.dot(a, b, preferred_element_type=F32)


def nothing(token_ref, out_ref):
    del token_ref, out_ref


def span(token, cost):
    return pl.pallas_call(
        nothing,
        out_shape=jax.ShapeDtypeStruct((8, 128), F32),
        in_specs=[ANY],
        out_specs=ANY,
        input_output_aliases={0: 0},
        cost_estimate=pl.CostEstimate(flops=cost, bytes_accessed=8192, transcendentals=0),
        compiler_params=pltpu.CompilerParams(has_side_effects=True, vmem_limit_bytes=2**16),
    )(token)


def hidden_kernel(tile, at_ref, *refs):
    *refs, out_ref = refs
    n = len(refs) // 3
    blocks, direct, swapped = refs[:n], refs[n : 2 * n], refs[2 * n :]
    rows, units = out_ref.shape
    gate_first = at_ref[1] == 1
    for shift in range(n):

        @pl.when(at_ref[0] == shift)
        def _(shift=shift):
            parts = [jnp.concatenate([direct[j][...], swapped[j][...]], axis=1) for j in range(n)]
            weights = jnp.concatenate(parts, axis=0)
            for r in range(0, rows, tile):
                cut = pl.ds(r, tile)
                sums = dot(jnp.concatenate([blocks[shift ^ j][cut, :] for j in range(n)], axis=1), weights)
                a, b = sums[:, :units], sums[:, units:]
                gate, up = jnp.where(gate_first, a, b), jnp.where(gate_first, b, a)
                out_ref[cut, :] = (gate / (1.0 + jnp.exp(-gate)) * up).astype(BF16)


def hidden_of(at, blocks, direct, swapped):
    rows, units = blocks[0].shape[0], direct[0].shape[1]
    size = sum(x.size for x in (*blocks, *direct, *swapped)) * 2
    return pl.pallas_call(
        functools.partial(hidden_kernel, rows // 2),
        out_shape=jax.ShapeDtypeStruct((rows, units), BF16),
        in_specs=[SMEM] + [VMEM] * (len(blocks) + len(direct) + len(swapped)),
        out_specs=VMEM,
        cost_estimate=pl.CostEstimate(flops=0, bytes_accessed=size, transcendentals=0),
        compiler_params=pltpu.CompilerParams(vmem_limit_bytes=16 * 2**20),
    )(at, *blocks, *direct, *swapped)


def output_kernel(at_ref, *refs):
    n = 4
    hidden, refs, out_ref = refs[:n], refs[n:-1], refs[-1]
    whole = [ref for ref in refs if ref.shape[0] == n]
    split = [ref for ref in refs if ref.shape[0] != n]
    split = list(zip(split[::2], split[1::2]))
    for shift in range(n):

        @pl.when(at_ref[1] == shift)
        def _(shift=shift):
            parts = []
            for i in range(n):
                part = [ref[at_ref[0] ^ i] for ref in whole]
                b = shift ^ i
                part += [pair[b // (n // 2)][b % (n // 2)] for pair in split]
                parts.append(jnp.concatenate(part, axis=1) if len(part) > 1 else part[0])
            rows = jnp.concatenate([ref[...] for ref in hidden], axis=1)
            out_ref[...] = dot(rows, jnp.concatenate(parts, axis=0)).astype(out_ref.dtype)


def output_of(at, hidden, down, kind):
    columns = sum(part.shape[2] * part.shape[0] for part in down) // len(hidden)
    size = sum(x.size for x in (*hidden, *down)) * 2
    return pl.pallas_call(
        output_kernel,
        out_shape=jax.ShapeDtypeStruct((hidden[0].shape[0], columns), kind),
        in_specs=[SMEM] + [VMEM] * (len(hidden) + len(down)),
        out_specs=VMEM,
        cost_estimate=pl.CostEstimate(flops=0, bytes_accessed=size, transcendentals=0),
        compiler_params=pltpu.CompilerParams(vmem_limit_bytes=16 * 2**20),
    )(at, *hidden, *down)


def add_kernel(columns, at_ref, mine_ref, theirs_ref, out_ref):
    for j in range(out_ref.shape[1] // columns):
        mine, theirs = (pl.ds(i * columns, columns) for i in (j, j ^ 1))
        cut = pl.ds(pl.multiple_of((at_ref[0] ^ j) * columns, columns), columns)
        out_ref[:, cut] = (mine_ref[:, mine] + theirs_ref[:, theirs]).astype(BF16)


def add(at, columns, mine, theirs):
    return pl.pallas_call(
        functools.partial(add_kernel, columns),
        out_shape=jax.ShapeDtypeStruct(mine.shape, BF16),
        in_specs=[SMEM] + [VMEM] * 2,
        out_specs=VMEM,
        compiler_params=pltpu.CompilerParams(vmem_limit_bytes=16 * 2**20),
    )(at, mine, theirs)


def shards(sizes, tokens, gate_weight, up_weight, down_weight):
    n_batch, n_weight = sizes[BATCH], sizes[WEIGHT]
    plane = lax.axis_index(BATCH)
    place = lax.axis_index(WEIGHT)
    first = lax.axis_index(GROUPS) == 0
    parity = plane % 2
    even = parity == 0
    rows = tokens.shape[0]
    half = gate_weight.shape[1] // 2
    columns = down_weight.shape[1]

    def flip(x, axis, bits):
        return lax.ppermute(x, axis, [(i, i ^ bits) for i in range(sizes[axis])])

    def half_of(weight, parity):
        return lax.dynamic_slice_in_dim(weight, parity * half, half, axis=1)

    def one_of(mine, theirs, parity):
        return jnp.where(first, half_of(mine, parity), half_of(theirs, parity))

    if n_batch == n_weight == 4:
        have = {N.tokens: tokens, N.gate_weight: gate_weight, N.up_weight: up_weight}
        have[N.send_own] = one_of(gate_weight, up_weight, parity)
        blocks = down_weight.reshape(n_weight, 2, half, columns)
        low, high = slice(0, n_weight // 2), slice(n_weight // 2, n_weight)

        def every(names):
            return [have[name] for name in names]

        def hidden(tokens):
            at = jnp.stack([place ^ plane, jnp.where(first, 1, 0)]).astype(jnp.int32)
            return hidden_of(at, every(tokens), every(DIRECT), every(SWAPPED))

        def output(hidden, kind):
            at = jnp.stack([place, place ^ jnp.where(first, 0, 2)]).astype(jnp.int32)
            return output_of(at, every(hidden), every(DOWN), kind)

        results = {
            N.send_other: lambda: one_of(have[N.gate_weight], have[N.up_weight], 1 - parity),
            N.keep_own: lambda: one_of(have[N.up_weight], have[N.gate_weight], parity),
            N.down_own: lambda: jnp.where(even, blocks[:, 0], blocks[:, 1]),
            N.down_other: lambda: jnp.where(even, blocks[:, 1], blocks[:, 0]),
            N.down_send_2: lambda: jnp.where(first, get(N.down_own)[low], get(N.down_own)[high]),
            N.down_send_3: lambda: jnp.where(first, get(N.down_other)[low], get(N.down_other)[high]),
            N.hidden_pair: lambda: hidden(PAIR),
            N.hidden_own: lambda: hidden(OWN),
            N.part: lambda: output(HIDDEN_PAIR, BF16),
            N.mine: lambda: output(HIDDEN_OWN, F32),
        }

        def get(name):
            if name not in have:
                have[name] = results[name]()
            return have[name]

        token = jnp.zeros((8, 128), F32)
        for arrived, leaving, cost in STAGES:
            sent = [TRANSFERS[name][0] for name in leaving]
            held = dict.fromkeys((*arrived, *sent))
            held = {name: get(name) for name in held if name in arrived or name not in LATE}
            if cost is not None:
                token, *values = lax.optimization_barrier((token, *held.values()))
                held = dict(zip(held, values))
                have.update((name, held[name]) for name in arrived)
                token = span(token, cost * 10**6)
            for name in leaving:
                source, *way = TRANSFERS[name]
                have[name] = flip(held[source] if source in held else get(source), *way)
        return add(plane.astype(jnp.int32).reshape(1), columns, have[N.mine], have[N.theirs])

    tokens_pair = flip(tokens, BATCH, 1)
    both = lax.all_gather(jnp.concatenate([tokens_pair, tokens], axis=0), WEIGHT, axis=1, tiled=True)
    mine = lax.all_gather(jnp.where(first, gate_weight, up_weight), BATCH, axis=0, tiled=True)
    mine = half_of(mine, parity)
    mine, theirs = dot(both, mine), dot(both, flip(mine, GROUPS, 1))
    gate_sum, up_sum = jnp.where(first, mine, theirs), jnp.where(first, theirs, mine)
    hidden = lax.all_gather((jax.nn.silu(gate_sum) * up_sum).astype(BF16), WEIGHT, axis=1, tiled=True)
    down_all = lax.all_gather(down_weight, BATCH, axis=1, tiled=True)
    down_all = down_all.reshape(n_weight, 2, half, n_batch * columns)
    down_all = jnp.where(even, down_all[:, 0], down_all[:, 1]).reshape(n_weight * half, n_batch * columns)
    theirs = flip(dot(hidden[:rows], down_all).astype(BF16), BATCH, 1)
    return (dot(hidden[rows:], down_all) + theirs).astype(BF16)


def solution(mesh):
    in_specs = (
        P((GROUPS, BATCH), WEIGHT),
        P(BATCH, WEIGHT),
        P(BATCH, WEIGHT),
        P(None, (WEIGHT, BATCH)),
    )
    out_specs = P((GROUPS, BATCH), WEIGHT)
    sizes = dict(mesh.shape)

    def body(*args):
        return shards(sizes, *args)

    return jax.shard_map(body, mesh=mesh, in_specs=in_specs, out_specs=out_specs, check_vma=False)
```

```python
import enum
import functools

import jax
import jax.numpy as jnp
from jax import lax
from jax.experimental import pallas as pl
from jax.experimental.pallas import tpu as pltpu
from jax.sharding import PartitionSpec as P

F32 = jnp.float32
BF16 = jnp.bfloat16
VMEM = pl.BlockSpec(memory_space=pltpu.VMEM)
SMEM = pl.BlockSpec(memory_space=pltpu.SMEM)
ANY = pl.BlockSpec(memory_space=pl.ANY)

BATCH, GROUPS, WEIGHT = "batch", "groups", "weight"


class N(enum.Enum):
    tokens = enum.auto()
    gate_weight = enum.auto()
    up_weight = enum.auto()
    send_own = enum.auto()
    send_other = enum.auto()
    keep_own = enum.auto()
    down_own = enum.auto()
    down_other = enum.auto()
    down_send_2 = enum.auto()
    down_send_3 = enum.auto()
    tokens_x = enum.auto()
    tokens_core = enum.auto()
    tokens_x_core = enum.auto()
    pair = enum.auto()
    pair_x = enum.auto()
    pair_core = enum.auto()
    pair_x_core = enum.auto()
    direct_1 = enum.auto()
    direct_2 = enum.auto()
    direct_3 = enum.auto()
    swapped_1 = enum.auto()
    swapped_2 = enum.auto()
    swapped_3 = enum.auto()
    down_1 = enum.auto()
    down_2 = enum.auto()
    down_3 = enum.auto()
    down_swapped_2 = enum.auto()
    down_swapped_3 = enum.auto()
    hidden_pair = enum.auto()
    hidden_pair_x = enum.auto()
    hidden_pair_core = enum.auto()
    hidden_pair_x_core = enum.auto()
    hidden_own = enum.auto()
    hidden_own_x = enum.auto()
    hidden_own_core = enum.auto()
    hidden_own_x_core = enum.auto()
    part = enum.auto()
    mine = enum.auto()
    theirs = enum.auto()


TRANSFERS = {
    N.tokens_x: (N.tokens, WEIGHT, 2),
    N.tokens_core: (N.tokens, WEIGHT, 1),
    N.tokens_x_core: (N.tokens_x, WEIGHT, 1),
    N.pair: (N.tokens, BATCH, 1),
    N.pair_x: (N.pair, WEIGHT, 2),
    N.pair_core: (N.pair, WEIGHT, 1),
    N.pair_x_core: (N.pair_x, WEIGHT, 1),
    N.direct_1: (N.send_other, BATCH, 1),
    N.direct_2: (N.send_own, BATCH, 2),
    N.direct_3: (N.send_other, BATCH, 3),
    N.swapped_1: (N.direct_1, GROUPS, 1),
    N.swapped_2: (N.direct_2, GROUPS, 1),
    N.swapped_3: (N.direct_3, GROUPS, 1),
    N.down_1: (N.down_other, BATCH, 1),
    N.down_2: (N.down_send_2, BATCH, 2),
    N.down_3: (N.down_send_3, BATCH, 3),
    N.down_swapped_2: (N.down_2, GROUPS, 1),
    N.down_swapped_3: (N.down_3, GROUPS, 1),
    N.hidden_pair_x: (N.hidden_pair, WEIGHT, 2),
    N.hidden_pair_core: (N.hidden_pair, WEIGHT, 1),
    N.hidden_pair_x_core: (N.hidden_pair_x, WEIGHT, 1),
    N.hidden_own_x: (N.hidden_own, WEIGHT, 2),
    N.hidden_own_core: (N.hidden_own, WEIGHT, 1),
    N.hidden_own_x_core: (N.hidden_own_x, WEIGHT, 1),
    N.theirs: (N.part, BATCH, 1),
}
PARTS = (N.keep_own, N.down_own, N.down_other, N.down_send_2, N.down_send_3)
LATE = (N.hidden_pair, N.hidden_own, N.part)
OWN = (N.tokens, N.tokens_core, N.tokens_x, N.tokens_x_core)
PAIR = (N.pair, N.pair_core, N.pair_x, N.pair_x_core)
HIDDEN_OWN = (N.hidden_own, N.hidden_own_core, N.hidden_own_x, N.hidden_own_x_core)
HIDDEN_PAIR = (N.hidden_pair, N.hidden_pair_core, N.hidden_pair_x, N.hidden_pair_x_core)
DIRECT = (N.send_own, N.direct_1, N.direct_2, N.direct_3)
SWAPPED = (N.keep_own, N.swapped_1, N.swapped_2, N.swapped_3)
DOWN = (N.down_own, N.down_1, N.down_2, N.down_swapped_2, N.down_3, N.down_swapped_3)
STAGES = (
    ((), (N.tokens_x, N.pair, N.tokens_core), None),
    ((N.gate_weight, N.up_weight), (N.direct_2,), 0),
    ((N.tokens_x, N.tokens_core), (N.direct_1,), 500),
    ((N.pair, N.direct_2), (N.direct_3, N.swapped_2, N.pair_x, N.tokens_x_core), 500),
    ((N.direct_1, *PARTS), (N.swapped_1,), 2600),
    ((N.swapped_2, N.tokens_x_core), (), 500),
    ((N.direct_3,), (N.swapped_3, N.pair_core, N.pair_x_core), 500),
    ((N.swapped_1, N.pair_x), (N.down_1, N.down_2), 2000),
    ((N.pair_core, N.pair_x_core), (N.down_3,), 500),
    ((N.swapped_3,), (N.hidden_pair_x,), 0),
    ((N.hidden_pair,), (), 0),
    ((N.down_2,), (N.down_swapped_2,), 500),
    ((N.down_1, N.down_3, N.hidden_own), (N.down_swapped_3,), 4500),
    ((N.hidden_pair_x,), (N.hidden_pair_core, N.hidden_pair_x_core, N.hidden_own_x), 500),
    ((N.down_swapped_2,), (), 500),
    ((N.down_swapped_3,), (), 3000),
    ((N.hidden_pair_core, N.hidden_pair_x_core), (N.theirs,), 2000),
    ((N.hidden_own_x,), (N.hidden_own_core, N.hidden_own_x_core), 500),
    ((N.hidden_own_core, N.hidden_own_x_core), (), 500),
    ((N.mine, N.theirs), (), 6000),
)


def dot(a, b):
    return jnp.dot(a, b, preferred_element_type=F32)


def nothing(token_ref, out_ref):
    del token_ref, out_ref


def span(token, cost):
    return pl.pallas_call(
        nothing,
        out_shape=jax.ShapeDtypeStruct((8, 128), F32),
        in_specs=[ANY],
        out_specs=ANY,
        input_output_aliases={0: 0},
        cost_estimate=pl.CostEstimate(flops=cost, bytes_accessed=8192, transcendentals=0),
        compiler_params=pltpu.CompilerParams(has_side_effects=True, vmem_limit_bytes=2**16),
    )(token)


def hidden_kernel(tile, at_ref, *refs):
    *refs, out_ref = refs
    n = len(refs) // 3
    blocks, direct, swapped = refs[:n], refs[n : 2 * n], refs[2 * n :]
    rows, units = out_ref.shape
    gate_first = at_ref[1] == 1
    for shift in range(n):

        @pl.when(at_ref[0] == shift)
        def _(shift=shift):
            parts = [jnp.concatenate([direct[j][...], swapped[j][...]], axis=1) for j in range(n)]
            weights = jnp.concatenate(parts, axis=0)
            for r in range(0, rows, tile):
                cut = pl.ds(r, tile)
                sums = dot(jnp.concatenate([blocks[shift ^ j][cut, :] for j in range(n)], axis=1), weights)
                a, b = sums[:, :units], sums[:, units:]
                gate, up = jnp.where(gate_first, a, b), jnp.where(gate_first, b, a)
                out_ref[cut, :] = (gate / (1.0 + jnp.exp(-gate)) * up).astype(BF16)


def hidden_of(at, blocks, direct, swapped):
    rows, units = blocks[0].shape[0], direct[0].shape[1]
    size = sum(x.size for x in (*blocks, *direct, *swapped)) * 2
    return pl.pallas_call(
        functools.partial(hidden_kernel, rows // 2),
        out_shape=jax.ShapeDtypeStruct((rows, units), BF16),
        in_specs=[SMEM] + [VMEM] * (len(blocks) + len(direct) + len(swapped)),
        out_specs=VMEM,
        cost_estimate=pl.CostEstimate(flops=0, bytes_accessed=size, transcendentals=0),
        compiler_params=pltpu.CompilerParams(vmem_limit_bytes=16 * 2**20),
    )(at, *blocks, *direct, *swapped)


def output_kernel(at_ref, *refs):
    n = 4
    hidden, refs, out_ref = refs[:n], refs[n:-1], refs[-1]
    whole = [ref for ref in refs if ref.shape[0] == n]
    split = [ref for ref in refs if ref.shape[0] != n]
    split = list(zip(split[::2], split[1::2]))
    for shift in range(n):

        @pl.when(at_ref[1] == shift)
        def _(shift=shift):
            parts = []
            for i in range(n):
                part = [ref[at_ref[0] ^ i] for ref in whole]
                b = shift ^ i
                part += [pair[b // (n // 2)][b % (n // 2)] for pair in split]
                parts.append(jnp.concatenate(part, axis=1) if len(part) > 1 else part[0])
            rows = jnp.concatenate([ref[...] for ref in hidden], axis=1)
            out_ref[...] = dot(rows, jnp.concatenate(parts, axis=0)).astype(out_ref.dtype)


def output_of(at, hidden, down, kind):
    columns = sum(part.shape[2] * part.shape[0] for part in down) // len(hidden)
    size = sum(x.size for x in (*hidden, *down)) * 2
    return pl.pallas_call(
        output_kernel,
        out_shape=jax.ShapeDtypeStruct((hidden[0].shape[0], columns), kind),
        in_specs=[SMEM] + [VMEM] * (len(hidden) + len(down)),
        out_specs=VMEM,
        cost_estimate=pl.CostEstimate(flops=0, bytes_accessed=size, transcendentals=0),
        compiler_params=pltpu.CompilerParams(vmem_limit_bytes=16 * 2**20),
    )(at, *hidden, *down)


def add_kernel(columns, at_ref, mine_ref, theirs_ref, out_ref):
    for j in range(out_ref.shape[1] // columns):
        mine, theirs = (pl.ds(i * columns, columns) for i in (j, j ^ 1))
        cut = pl.ds(pl.multiple_of((at_ref[0] ^ j) * columns, columns), columns)
        out_ref[:, cut] = (mine_ref[:, mine] + theirs_ref[:, theirs]).astype(BF16)


def add(at, columns, mine, theirs):
    return pl.pallas_call(
        functools.partial(add_kernel, columns),
        out_shape=jax.ShapeDtypeStruct(mine.shape, BF16),
        in_specs=[SMEM] + [VMEM] * 2,
        out_specs=VMEM,
        compiler_params=pltpu.CompilerParams(vmem_limit_bytes=16 * 2**20),
    )(at, mine, theirs)


def shards(sizes, tokens, gate_weight, up_weight, down_weight):
    n_batch, n_weight = sizes[BATCH], sizes[WEIGHT]
    plane = lax.axis_index(BATCH)
    place = lax.axis_index(WEIGHT)
    first = lax.axis_index(GROUPS) == 0
    parity = plane % 2
    even = parity == 0
    rows = tokens.shape[0]
    half = gate_weight.shape[1] // 2
    columns = down_weight.shape[1]

    def flip(x, axis, bits):
        return lax.ppermute(x, axis, [(i, i ^ bits) for i in range(sizes[axis])])

    def half_of(weight, parity):
        return lax.dynamic_slice_in_dim(weight, parity * half, half, axis=1)

    def one_of(mine, theirs, parity):
        return jnp.where(first, half_of(mine, parity), half_of(theirs, parity))

    if n_batch == n_weight == 4:
        have = {N.tokens: tokens, N.gate_weight: gate_weight, N.up_weight: up_weight}
        have[N.send_own] = one_of(gate_weight, up_weight, parity)
        blocks = down_weight.reshape(n_weight, 2, half, columns)
        low, high = slice(0, n_weight // 2), slice(n_weight // 2, n_weight)

        def every(names):
            return [have[name] for name in names]

        def hidden(tokens):
            at = jnp.stack([place ^ plane, jnp.where(first, 1, 0)]).astype(jnp.int32)
            return hidden_of(at, every(tokens), every(DIRECT), every(SWAPPED))

        def output(hidden, kind):
            at = jnp.stack([place, place ^ jnp.where(first, 0, 2)]).astype(jnp.int32)
            return output_of(at, every(hidden), every(DOWN), kind)

        results = {
            N.send_other: lambda: one_of(have[N.gate_weight], have[N.up_weight], 1 - parity),
            N.keep_own: lambda: one_of(have[N.up_weight], have[N.gate_weight], parity),
            N.down_own: lambda: jnp.where(even, blocks[:, 0], blocks[:, 1]),
            N.down_other: lambda: jnp.where(even, blocks[:, 1], blocks[:, 0]),
            N.down_send_2: lambda: jnp.where(first, get(N.down_own)[low], get(N.down_own)[high]),
            N.down_send_3: lambda: jnp.where(first, get(N.down_other)[low], get(N.down_other)[high]),
            N.hidden_pair: lambda: hidden(PAIR),
            N.hidden_own: lambda: hidden(OWN),
            N.part: lambda: output(HIDDEN_PAIR, BF16),
            N.mine: lambda: output(HIDDEN_OWN, F32),
        }

        def get(name):
            if name not in have:
                have[name] = results[name]()
            return have[name]

        token = jnp.zeros((8, 128), F32)
        for arrived, leaving, cost in STAGES:
            sent = [TRANSFERS[name][0] for name in leaving]
            held = dict.fromkeys((*arrived, *sent))
            held = {name: get(name) for name in held if name in arrived or name not in LATE}
            if cost is not None:
                token, *values = lax.optimization_barrier((token, *held.values()))
                held = dict(zip(held, values))
                have.update((name, held[name]) for name in arrived)
                token = span(token, cost * 10**6)
            for name in leaving:
                source, *way = TRANSFERS[name]
                have[name] = flip(held[source] if source in held else get(source), *way)
        return add(plane.astype(jnp.int32).reshape(1), columns, have[N.mine], have[N.theirs])

    tokens_pair = flip(tokens, BATCH, 1)
    both = lax.all_gather(jnp.concatenate([tokens_pair, tokens], axis=0), WEIGHT, axis=1, tiled=True)
    mine = lax.all_gather(jnp.where(first, gate_weight, up_weight), BATCH, axis=0, tiled=True)
    mine = half_of(mine, parity)
    mine, theirs = dot(both, mine), dot(both, flip(mine, GROUPS, 1))
    gate_sum, up_sum = jnp.where(first, mine, theirs), jnp.where(first, theirs, mine)
    hidden = lax.all_gather((jax.nn.silu(gate_sum) * up_sum).astype(BF16), WEIGHT, axis=1, tiled=True)
    down_all = lax.all_gather(down_weight, BATCH, axis=1, tiled=True)
    down_all = down_all.reshape(n_weight, 2, half, n_batch * columns)
    down_all = jnp.where(even, down_all[:, 0], down_all[:, 1]).reshape(n_weight * half, n_batch * columns)
    theirs = flip(dot(hidden[:rows], down_all).astype(BF16), BATCH, 1)
    return (dot(hidden[rows:], down_all) + theirs).astype(BF16)


def solution(mesh):
    in_specs = (
        P((GROUPS, BATCH), WEIGHT),
        P(BATCH, WEIGHT),
        P(BATCH, WEIGHT),
        P(None, (WEIGHT, BATCH)),
    )
    out_specs = P((GROUPS, BATCH), WEIGHT)
    sizes = dict(mesh.shape)

    def body(*args):
        return shards(sizes, *args)

    return jax.shard_map(body, mesh=mesh, in_specs=in_specs, out_specs=out_specs, check_vma=False)
```
